32 devices in a mesh: fsdp: 16 (over z, y, x), dp: 2 (over core).
Axes of the slice: x: 2, y: 2, z: 4, core: 2. Of those that a mesh axis runs over, the one named last changes fastest.
Arguments:
- tokens: bfloat16 [2, 16384, 1024], P(None, ('fsdp', 'dp')), may hold values from -6 to 6
- cotangent: bfloat16 [2, 16384, 1024], P(None, ('fsdp', 'dp')), may hold values from -6 to 6
- lengths: int32 [2, 128], P(None, ('fsdp', 'dp')), may hold values from 0 to 512, as said below
- qkv_weight: float32 [1024, 3072], P('fsdp'), may hold values from -0.1875 to 0.1875
- dense_weight: float32 [1024, 1024], P('fsdp'), may hold values from -0.5 to 0.5
- expand_weight: float32 [1024, 4096], P('fsdp'), may hold values from -0.1875 to 0.1875
- contract_weight: float32 [4096, 1024], P('fsdp'), may hold values from -0.09375 to 0.09375
- vectors: float32 [13312], P('fsdp'), may hold values from -1.2 to 2
- qkv_first: float32 [1024, 3072], P('fsdp'), may hold values from -128 to 128
- dense_first: float32 [1024, 1024], P('fsdp'), may hold values from -32 to 32
- expand_first: float32 [1024, 4096], P('fsdp'), may hold values from -24 to 24
- contract_first: float32 [4096, 1024], P('fsdp'), may hold values from -48 to 48
- vector_first: float32 [13312], P('fsdp'), may hold values from -128 to 128
- qkv_second: float32 [1024, 3072], P('fsdp'), may hold values from 1723.5968 to 6881.28
- dense_second: float32 [1024, 1024], P('fsdp'), may hold values from 155.32031 to 619.3152
- expand_second: float32 [1024, 4096], P('fsdp'), may hold values from 68.8128 to 275.2512
- contract_second: float32 [4096, 1024], P('fsdp'), may hold values from 275.2512 to 1104.2816
- vector_second: float32 [13312], P('fsdp'), may hold values from 1723.5968 to 6881.28
Outputs:
- output: bfloat16 [2, 16384, 1024], P(None, ('fsdp', 'dp'))
- input_grad: float32 [2, 16384, 1024], P(None, ('fsdp', 'dp'))
- qkv_new: float32 [1024, 3072], P('fsdp')
- dense_new: float32 [1024, 1024], P('fsdp')
- expand_new: float32 [1024, 4096], P('fsdp')
- contract_new: float32 [4096, 1024], P('fsdp')
- vectors_new: float32 [13312], P('fsdp')
- qkv_first_new: float32 [1024, 3072], P('fsdp')
- dense_first_new: float32 [1024, 1024], P('fsdp')
- expand_first_new: float32 [1024, 4096], P('fsdp')
- contract_first_new: float32 [4096, 1024], P('fsdp')
- vector_first_new: float32 [13312], P('fsdp')
- qkv_second_new: float32 [1024, 3072], P('fsdp')
- dense_second_new: float32 [1024, 1024], P('fsdp')
- expand_second_new: float32 [1024, 4096], P('fsdp')
- contract_second_new: float32 [4096, 1024], P('fsdp')
- vector_second_new: float32 [13312], P('fsdp')
The draws below stay inside these ranges and needn't reach their ends.
Inputs may be any that keep to these rules, and one draw needn't show every extreme that they name: In each micro-batch the 4 lengths of every block sum to 256 or more and to at most 512; in some block of some micro-batch a single sequence fills all 512 rows.
All inputs are finite; a program needn't handle non-finite values.
Results may differ from the reference program's by a relative error of at most 0.017.
The reference program's roundings to bfloat16 on the way count: a program that leaves them out, or rounds other values in their place, can miss the bound.
Values may be sent and summed in bfloat16 or wider, within the bound.
A program may use at most 256 MiB of HBM per device.

```python
import math
import jax
import jax.numpy as jnp
from jax import lax

HEADS = 16
HEAD_DIM = 64
D = 1024
FF = 4096
ROWS = 512
SEQS = 4
MICRO = 2
STEP = 10
VEC = 13312
ALLROWS = 16384
TOKENS = 32768


def draw_lengths(key, part):
    key = jax.random.fold_in(key, 11)
    block_count = MICRO * ALLROWS // ROWS
    key_fill, key_cut, key_full = jax.random.split(key, 3)
    filled = jax.random.randint(key_fill, (block_count, 1), ROWS // 2, ROWS + 1).astype(jnp.int32)
    cut_points = jnp.sort(jax.random.randint(key_cut, (block_count, SEQS - 1), 0, ROWS + 1).astype(jnp.int32), axis=1)
    inner_cuts = cut_points * filled // ROWS
    cut_edges = jnp.concatenate([jnp.zeros((block_count, 1), jnp.int32), inner_cuts, filled], axis=1)
    seq_lengths = cut_edges[:, 1:] - cut_edges[:, :-1]
    chosen = jax.random.randint(key_full, (), 0, block_count)
    single = jnp.where(jnp.arange(SEQS) == 0, ROWS, 0).astype(jnp.int32)
    picked = (jnp.arange(block_count) == chosen)[:, None]
    seq_lengths = jnp.where(picked, single[None, :], seq_lengths)
    return seq_lengths.reshape(MICRO, block_count // MICRO * SEQS).astype(jnp.int32)


def draw_vectors(key, part):
    key = jax.random.fold_in(key, 23)
    key_gain, key_shift = jax.random.split(key)
    positions = jnp.arange(VEC)
    is_gain = (positions < D) | (positions >= 6 * D) & (positions < 7 * D)
    gain_values = 0.5 + 1.5 * jax.random.uniform(key_gain, (VEC,), jnp.float32)
    shifts = 0.3 * jax.random.truncated_normal(key_shift, -4.0, 4.0, (VEC,), jnp.float32)
    return jnp.where(is_gain, gain_values, shifts).astype(jnp.float32)


def levels(own_key, dims, pieces, least, largest):
    def one(axis_at, parts):
        draws = jax.random.uniform(jax.random.fold_in(jax.random.fold_in(own_key, 6), axis_at), (parts,), jnp.float32, least / len(pieces), largest / len(pieces))
        return jnp.repeat(jnp.exp(draws), dims[axis_at] // parts).reshape((-1,) + (1,) * (len(dims) - axis_at - 1))

    loudness = one(*pieces[0])
    for cut in pieces[1:]:
        loudness = loudness * one(*cut)
    return loudness


def normal_values(rng, shape, width, reach, cuts=(), held_as=jnp.bfloat16):
    gain = levels(rng, shape, cuts, -0.22, 0.18) if cuts else 1.0
    values = jax.random.normal(rng, shape, jnp.float32) * width * gain
    return jnp.minimum(jnp.maximum(values, -reach), reach).astype(held_as)


def setup_inputs(seed: int = 0) -> dict:
    seeds = jax.random.split(jax.random.key(seed), 19)
    tokens = normal_values(seeds[0], (MICRO, ALLROWS, D), 1.0, 6.0, ((1, 32),))
    cotangent = normal_values(seeds[1], (MICRO, ALLROWS, D), 1.0, 6.0, ((1, 32),))
    lengths = draw_lengths(jax.random.fold_in(seeds[18], 71), 0)
    qkv_weight = normal_values(seeds[3], (D, 3 * D), D ** -0.5, 0.1875, ((0, 16),), jnp.float32)
    dense_weight = normal_values(seeds[4], (D, D), (D // 8) ** -0.5, 0.5, ((0, 16),), jnp.float32)
    expand_weight = normal_values(seeds[5], (D, FF), D ** -0.5, 0.1875, ((0, 16),), jnp.float32)
    contract_weight = normal_values(seeds[6], (FF, D), FF ** -0.5, 0.09375, ((0, 16),), jnp.float32)
    vectors = draw_vectors(jax.random.fold_in(seeds[18], 71), 0)
    qkv_first = normal_values(seeds[8], (D, 3 * D), (0.111 * TOKENS ** 0.5), 128.0, ((0, 16),), jnp.float32)
    dense_first = normal_values(seeds[9], (D, D), (0.0333 * TOKENS ** 0.5), 32.0, ((0, 16),), jnp.float32)
    expand_first = normal_values(seeds[10], (D, FF), (0.0222 * TOKENS ** 0.5), 24.0, ((0, 16),), jnp.float32)
    contract_first = normal_values(seeds[11], (FF, D), (0.0444 * TOKENS ** 0.5), 48.0, ((0, 16),), jnp.float32)
    vector_first = normal_values(seeds[12], (VEC,), (0.111 * TOKENS ** 0.5), 128.0, ((0, 16),), jnp.float32)
    qkv_second = jnp.clip(jnp.exp(math.log(6881.28) - 1.3843914 * jax.random.uniform(seeds[13], (D, 3 * D), jnp.float32) ** levels(seeds[13], (D, 3 * D), ((0, 16),), -0.2, 0.2)), 1723.5968, 6881.28)
    dense_second = jnp.clip(jnp.exp(math.log(619.3152) - 1.3831248 * jax.random.uniform(seeds[14], (D, D), jnp.float32) ** levels(seeds[14], (D, D), ((0, 16),), -0.2, 0.2)), 155.32031, 619.3152)
    expand_second = jnp.clip(jnp.exp(math.log(275.2512) - 1.3862944 * jax.random.uniform(seeds[15], (D, FF), jnp.float32) ** levels(seeds[15], (D, FF), ((0, 16),), -0.2, 0.2)), 68.8128, 275.2512)
    contract_second = jnp.clip(jnp.exp(math.log(1104.2816) - 1.38926618 * jax.random.uniform(seeds[16], (FF, D), jnp.float32) ** levels(seeds[16], (FF, D), ((0, 16),), -0.2, 0.2)), 275.2512, 1104.2816)
    vector_second = jnp.clip(jnp.exp(math.log(6881.28) - 1.3843914 * jax.random.uniform(seeds[17], (VEC,), jnp.float32) ** levels(seeds[17], (VEC,), ((0, 16),), -0.2, 0.2)), 1723.5968, 6881.28)
    return dict(tokens=tokens, cotangent=cotangent, lengths=lengths, qkv_weight=qkv_weight, dense_weight=dense_weight, expand_weight=expand_weight, contract_weight=contract_weight, vectors=vectors, qkv_first=qkv_first, dense_first=dense_first, expand_first=expand_first, contract_first=contract_first, vector_first=vector_first, qkv_second=qkv_second, dense_second=dense_second, expand_second=expand_second, contract_second=contract_second, vector_second=vector_second)


norm_eps = 1e-05
beta_first = 0.9
beta_second = 0.95
adam_eps = 1e-08
matrix_rate = 0.05
vector_rate = 0.5
decay_rate = 0.1
masked_score = -1e+30

@jax.custom_vjp
def low(v):
    return lax.optimization_barrier(v.astype(jnp.bfloat16)).astype(jnp.float32)

@jax.custom_vjp
def low_back(v):
    return v

def low_keep(v):
    return (low(v), None)

def low_pass(kept, grad):
    return (grad,)

def back_keep(v):
    return (v, None)

def back_low(kept, grad):
    return (low(grad),)
low.defvjp(low_keep, low_pass)
low_back.defvjp(back_keep, back_low)

def matmul(left_side, right_side):
    return jnp.dot(left_side, right_side, precision=lax.Precision.HIGHEST, preferred_element_type=jnp.float32)

def normalize(inputs, norm_gain, norm_shift):
    average = lax.optimization_barrier(jnp.mean(inputs, axis=-1, keepdims=True))
    centered = inputs - average
    spread = lax.optimization_barrier(jnp.mean(centered * centered, axis=-1, keepdims=True))
    return centered * lax.rsqrt(spread + norm_eps) * norm_gain + norm_shift

def segment_rows(lengths_row, row_count):
    bounds = jnp.cumsum(lengths_row).astype(jnp.int32)
    row_ids = jnp.arange(row_count, dtype=jnp.int32)
    segment = lax.optimization_barrier(jnp.sum((row_ids[:, None] >= bounds[None, :]).astype(jnp.int32), axis=1))
    inside = (row_ids < bounds[-1]).astype(jnp.float32)
    return (segment, inside)

def head_slopes():
    return 2.0 ** (-8.0 * (jnp.arange(HEADS, dtype=jnp.float32) + 1.0) / HEADS)

def block_layer(params, inputs, segment):
    joined_mat, dense_mat, expand_mat, contract_mat, vector_low = [low(parameter) for parameter in params]
    gain_one = vector_low[0:D]
    shift_one = vector_low[D:2 * D]
    qkv_bias = vector_low[2 * D:5 * D]
    dense_bias = vector_low[5 * D:6 * D]
    gain_two = vector_low[6 * D:7 * D]
    shift_two = vector_low[7 * D:8 * D]
    expand_bias = vector_low[8 * D:8 * D + FF]
    contract_bias = vector_low[8 * D + FF:9 * D + FF]
    row_count = inputs.shape[0]
    first_norm = low(normalize(inputs, gain_one, shift_one))
    projected = low(low_back(matmul(first_norm, joined_mat) + qkv_bias))
    queries = projected[:, :D].reshape(row_count, HEADS, HEAD_DIM)
    keys_all = projected[:, D:2 * D].reshape(row_count, HEADS, HEAD_DIM)
    values_all = projected[:, 2 * D:].reshape(row_count, HEADS, HEAD_DIM)
    raw_scores = jnp.einsum('qhd,khd->hqk', queries, keys_all, precision=lax.Precision.HIGHEST) * HEAD_DIM ** (-0.5)
    row_ids = jnp.arange(row_count, dtype=jnp.int32)
    distance = (row_ids[:, None] - row_ids[None, :]).astype(jnp.float32)
    raw_scores = raw_scores - head_slopes()[:, None, None] * distance[None]
    scores = low_back(raw_scores)
    allowed = (segment[:, None] == segment[None, :]) & (row_ids[None, :] <= row_ids[:, None])
    scores = jnp.where(allowed[None], scores, masked_score)
    probability = low(jax.nn.softmax(scores, axis=-1))
    context = jnp.einsum('hqk,khd->qhd', probability, values_all, precision=lax.Precision.HIGHEST).reshape(row_count, D)
    context = low(low_back(context))
    residual_one = inputs + (low_back(matmul(context, dense_mat)) + dense_bias)
    second_norm = low(normalize(residual_one, gain_two, shift_two))
    expanded = low_back(matmul(second_norm, expand_mat) + expand_bias)
    activated = low(jax.nn.gelu(expanded, approximate=True))
    return residual_one + (matmul(activated, contract_mat) + contract_bias)

def add_pair(first_term, second_term):
    return first_term + second_term

def adam_update(weight, first, second, grad, rate, decay):
    new_first = beta_first * first + (1.0 - beta_first) * grad
    new_second = beta_second * second + (1.0 - beta_second) * grad * grad
    corrected_first = new_first / (1.0 - beta_first ** STEP)
    corrected_second = new_second / (1.0 - beta_second ** STEP)
    new_weight = weight - rate * (corrected_first / (jnp.sqrt(corrected_second) + adam_eps) + decay * weight)
    return (new_weight, new_first, new_second)

def reference(tokens, cotangent, lengths, qkv_weight, dense_weight, expand_weight, contract_weight, vectors, qkv_first, dense_first, expand_first, contract_first, vector_first, qkv_second, dense_second, expand_second, contract_second, vector_second):
    block_count = MICRO * ALLROWS // ROWS
    token_blocks = tokens.astype(jnp.float32).reshape(block_count, ROWS, D)
    upstream_blocks = cotangent.astype(jnp.float32).reshape(block_count, ROWS, D)
    length_blocks = lengths.reshape(block_count, SEQS)
    params = (qkv_weight, dense_weight, expand_weight, contract_weight, vectors)

    def one_block(totals, block_data):
        inputs, upstream, lengths_row = block_data
        segment, inside = segment_rows(lengths_row, ROWS)

        def layer_apply(weight_set, activations):
            return block_layer(weight_set, activations, segment)
        result, backward = jax.vjp(layer_apply, params, inputs)
        grad_params, grad_inputs = backward(upstream * inside[:, None])
        totals = jax.tree.map(add_pair, totals, grad_params)
        return (totals, (result.astype(jnp.bfloat16), grad_inputs))
    zero_grads = tuple((jnp.zeros_like(parameter) for parameter in params))
    grad_sums, (results, input_grads) = lax.scan(one_block, zero_grads, (token_blocks, upstream_blocks, length_blocks))
    output = results.reshape(MICRO, ALLROWS, D)
    input_grad = input_grads.reshape(MICRO, ALLROWS, D)
    qkv_new, qkv_first_new, qkv_second_new = adam_update(qkv_weight, qkv_first, qkv_second, grad_sums[0], matrix_rate, decay_rate)
    dense_new, dense_first_new, dense_second_new = adam_update(dense_weight, dense_first, dense_second, grad_sums[1], matrix_rate, decay_rate)
    expand_new, expand_first_new, expand_second_new = adam_update(expand_weight, expand_first, expand_second, grad_sums[2], matrix_rate, decay_rate)
    contract_new, contract_first_new, contract_second_new = adam_update(contract_weight, contract_first, contract_second, grad_sums[3], matrix_rate, decay_rate)
    vectors_new, vector_first_new, vector_second_new = adam_update(vectors, vector_first, vector_second, grad_sums[4], vector_rate, 0.0)
    return (output, input_grad, qkv_new, dense_new, expand_new, contract_new, vectors_new, qkv_first_new, dense_first_new, expand_first_new, contract_first_new, vector_first_new, qkv_second_new, dense_second_new, expand_second_new, contract_second_new, vector_second_new)
```

```python
import functools

import jax
import jax.numpy as jnp
from jax import lax
from jax.experimental import pallas as pl
from jax.experimental.pallas import tpu as pltpu
from jax.sharding import PartitionSpec as P

HEADS = 16
HEAD_DIM = 64
D = 1024
FF = 4096
STEP = 10
VEC = 13312

norm_eps = 1e-05
beta_first = 0.9
beta_second = 0.95
adam_eps = 1e-08
matrix_rate = 0.05
vector_rate = 0.5
decay_rate = 0.1
excluded = 1e33
TILE = 256
PAIR = 2


def pieces(vector):
    return (
        vector[0:D],
        vector[D : 2 * D],
        vector[2 * D : 5 * D],
        vector[5 * D : 6 * D],
        vector[6 * D : 7 * D],
        vector[7 * D : 8 * D],
        vector[8 * D : 8 * D + FF],
        vector[8 * D + FF : 9 * D + FF],
    )


def product(left_side, right_side):
    return jnp.dot(left_side, right_side, preferred_element_type=jnp.float32)


def outer_sum(left_side, right_side):
    return lax.dot_general(
        left_side, right_side, (((0,), (0,)), ((), ())), preferred_element_type=jnp.float32
    )


def times_transposed(left_side, right_side):
    return lax.dot_general(
        left_side, right_side, (((1,), (1,)), ((), ())), preferred_element_type=jnp.float32
    )


def norm_parts(inputs):
    average = jnp.mean(inputs, axis=-1, keepdims=True)
    centered = inputs - average
    spread = jnp.mean(centered * centered, axis=-1, keepdims=True)
    scale = lax.rsqrt(spread + norm_eps)
    return centered * scale, scale


def norm_back(unit, scale, gain, upstream):
    by_gain = upstream * gain
    mean_one = jnp.mean(by_gain, axis=-1, keepdims=True)
    mean_two = jnp.mean(by_gain * unit, axis=-1, keepdims=True)
    return scale * (by_gain - mean_one - unit * mean_two)


def gelu_both(values):
    root = 0.7978845608028654
    square = values * values
    bent = jnp.tanh(root * values * (1.0 + 0.044715 * square))
    half = 0.5 * (1.0 + bent)
    slope = half + 0.5 * values * (1.0 - bent * bent) * root * (1.0 + 3 * 0.044715 * square)
    return values * half, slope


def slope_of(head):
    return jnp.exp2(-8.0 * (head.astype(jnp.float32) + 1.0) / HEADS)


def fill_distance(seg_col, seg_row, distance_ref):
    rows = distance_ref.shape[0]
    key_rows = lax.broadcasted_iota(jnp.int32, (rows, rows), 0)
    query_rows = lax.broadcasted_iota(jnp.int32, (rows, rows), 1)
    allowed = (seg_col == seg_row) & (key_rows <= query_rows)
    distance_ref[...] = jnp.where(allowed, (query_rows - key_rows).astype(jnp.float32), excluded)


def attend_kernel(seg_col, seg_row, q_ref, k_ref, v_ref, out_ref, stat_ref, distance_ref):
    step = pl.program_id(1)

    @pl.when(step == 0)
    def _():
        fill_distance(seg_col[0], seg_row[0], distance_ref)

    rows = q_ref.shape[0]
    queries = q_ref[...] * jnp.bfloat16(HEAD_DIM**-0.5)
    values_turned = v_ref[...].T
    for local_head in range(PAIR):
        slope = slope_of(step * PAIR + local_head)
        lanes = slice(local_head * HEAD_DIM, (local_head + 1) * HEAD_DIM)
        for tile in range(rows // TILE):
            high = (tile + 1) * TILE
            span = slice(tile * TILE, high)
            scores = times_transposed(k_ref[:high, lanes], queries[span, lanes])
            scores = scores - slope * distance_ref[:high, span]
            top = jnp.max(scores, axis=0, keepdims=True)
            exponent = jnp.exp(scores - top)
            total = jnp.sum(exponent, axis=0, keepdims=True)
            probability = (exponent * (1.0 / total)).astype(jnp.bfloat16)
            turned = product(values_turned[lanes, :high], probability)
            out_ref[span, lanes] = turned.T.astype(jnp.bfloat16)
            stat_ref[0, local_head : local_head + 1, span] = top + jnp.log(total)


def attend_back_kernel(
    seg_col, seg_row, q_ref, k_ref, v_ref, up_ref, stat_ref, dq_ref, dk_ref, dv_ref,
    distance_ref, sum_k, sum_v,
):
    step = pl.program_id(1)

    @pl.when(step == 0)
    def _():
        fill_distance(seg_col[0], seg_row[0], distance_ref)

    rows = q_ref.shape[0]
    queries = q_ref[...] * jnp.bfloat16(HEAD_DIM**-0.5)
    upstream = up_ref[...]
    keys_turned = k_ref[...].T
    for local_head in range(PAIR):
        slope = slope_of(step * PAIR + local_head)
        lanes = slice(local_head * HEAD_DIM, (local_head + 1) * HEAD_DIM)
        for tile in range(rows // TILE):
            high = (tile + 1) * TILE
            span = slice(tile * TILE, high)
            scores = times_transposed(k_ref[:high, lanes], queries[span, lanes])
            scores = scores - slope * distance_ref[:high, span]
            probability = jnp.exp(scores - stat_ref[0, local_head : local_head + 1, span])
            grad_probs = times_transposed(v_ref[:high, lanes], upstream[span, lanes])
            weighted = probability * grad_probs
            correction = jnp.sum(weighted, axis=0, keepdims=True)
            grad_scores = (weighted - probability * correction).astype(jnp.bfloat16)
            grad_query = product(keys_turned[lanes, :high], grad_scores)
            dq_ref[span, lanes] = (grad_query.T * HEAD_DIM**-0.5).astype(jnp.bfloat16)
            part_k = product(grad_scores, queries[span, lanes])
            part_v = product(probability.astype(jnp.bfloat16), upstream[span, lanes])
            if tile == 0:
                sum_k[:high, lanes] = part_k
                sum_v[:high, lanes] = part_v
            else:
                low = tile * TILE
                sum_k[:low, lanes] += part_k[:low]
                sum_v[:low, lanes] += part_v[:low]
                sum_k[low:high, lanes] = part_k[low:]
                sum_v[low:high, lanes] = part_v[low:]
    dk_ref[...] = sum_k[...].astype(jnp.bfloat16)
    dv_ref[...] = sum_v[...].astype(jnp.bfloat16)


def attention_specs(rows, blocks):
    steps = HEADS // PAIR
    width = PAIR * HEAD_DIM
    seg_specs = [
        pl.BlockSpec((1, rows, 1), lambda b, s: (b, 0, 0)),
        pl.BlockSpec((1, 1, rows), lambda b, s: (b, 0, 0)),
    ]

    def part(which):
        return pl.BlockSpec((rows, width), lambda b, s: (b, s + which * steps))

    stat = pl.BlockSpec((1, PAIR, rows), lambda b, s: (b * steps + s, 0, 0))
    return steps, seg_specs, part, stat


def attend(projected, segment):
    blocks, rows = segment.shape
    steps, seg_specs, part, stat = attention_specs(rows, blocks)
    return pl.pallas_call(
        attend_kernel,
        grid=(blocks, steps),
        in_specs=seg_specs + [part(0), part(1), part(2)],
        out_specs=[part(0), stat],
        out_shape=[
            jax.ShapeDtypeStruct((blocks * rows, D), jnp.bfloat16),
            jax.ShapeDtypeStruct((blocks * steps, PAIR, rows), jnp.float32),
        ],
        scratch_shapes=[pltpu.VMEM((rows, rows), jnp.float32)],
        compiler_params=pltpu.CompilerParams(vmem_limit_bytes=32 * 2**20),
        cost_estimate=pl.CostEstimate(
            flops=blocks * HEADS * rows * rows * HEAD_DIM * 8,
            bytes_accessed=blocks * rows * D * 8,
            transcendentals=blocks * HEADS * rows * rows,
        ),
        name="attend",
    )(segment[:, :, None], segment[:, None, :], projected, projected, projected)


def attend_back(projected, upstream, stats, segment):
    blocks, rows = segment.shape
    steps, seg_specs, part, stat = attention_specs(rows, blocks)
    width = PAIR * HEAD_DIM
    return pl.pallas_call(
        attend_back_kernel,
        grid=(blocks, steps),
        in_specs=seg_specs + [part(0), part(1), part(2), part(0), stat],
        out_specs=[part(0), part(0), part(0)],
        out_shape=[jax.ShapeDtypeStruct((blocks * rows, D), jnp.bfloat16)] * 3,
        scratch_shapes=[
            pltpu.VMEM((rows, rows), jnp.float32),
            pltpu.VMEM((rows, width), jnp.float32),
            pltpu.VMEM((rows, width), jnp.float32),
        ],
        compiler_params=pltpu.CompilerParams(vmem_limit_bytes=32 * 2**20),
        cost_estimate=pl.CostEstimate(
            flops=blocks * HEADS * rows * rows * HEAD_DIM * 20,
            bytes_accessed=blocks * rows * D * 14,
            transcendentals=blocks * HEADS * rows * rows,
        ),
        name="attend_back",
    )(segment[:, :, None], segment[:, None, :], projected, projected, projected, upstream, stats)


def adam_update(weight, first, second, grad, rate, decay):
    new_first = beta_first * first + (1.0 - beta_first) * grad
    new_second = beta_second * second + (1.0 - beta_second) * grad * grad
    corrected_first = new_first / (1.0 - beta_first**STEP)
    corrected_second = new_second / (1.0 - beta_second**STEP)
    new_weight = weight - rate * (
        corrected_first / (jnp.sqrt(corrected_second) + adam_eps) + decay * weight
    )
    return (new_weight, new_first, new_second)


def gather(own):
    copies = lax.axis_size("dp")
    share = own.shape[0] // copies
    mine = lax.dynamic_slice_in_dim(own, lax.axis_index("dp") * share, share, 0)
    return lax.all_gather(mine.astype(jnp.bfloat16), ("fsdp", "dp"), axis=0, tiled=True)


def scatter(total):
    part = lax.psum_scatter(
        total.astype(jnp.bfloat16), ("fsdp", "dp"), scatter_dimension=0, tiled=True
    )
    return lax.all_gather(part, "dp", axis=0, tiled=True).astype(jnp.float32)


def local(
    tokens,
    cotangent,
    lengths,
    qkv_weight,
    dense_weight,
    expand_weight,
    contract_weight,
    vectors,
    qkv_first,
    dense_first,
    expand_first,
    contract_first,
    vector_first,
    qkv_second,
    dense_second,
    expand_second,
    contract_second,
    vector_second,
):
    batches, row_count, _ = tokens.shape
    rows = batches * row_count
    bounds = jnp.cumsum(lengths, axis=1)
    row_ids = jnp.arange(row_count, dtype=jnp.int32)
    segment = jnp.sum((row_ids[None, :, None] >= bounds[:, None, :]).astype(jnp.int32), axis=2)
    inside = (row_ids[None, :] < bounds[:, -1:]).reshape(rows, 1)

    vector_all = gather(vectors)
    qkv_mat = gather(qkv_weight)
    dense_mat = gather(dense_weight)
    expand_mat = gather(expand_weight)
    contract_mat = gather(contract_weight)
    (
        gain_one, shift_one, qkv_bias, dense_bias, gain_two, shift_two, expand_bias, contract_bias,
    ) = pieces(vector_all.astype(jnp.float32))

    inputs = tokens.reshape(rows, D).astype(jnp.float32)
    grad_low = jnp.where(inside, cotangent.reshape(rows, D), jnp.bfloat16(0))
    grad_out = grad_low.astype(jnp.float32)

    unit_one, scale_one = norm_parts(inputs)
    first_norm = (unit_one * gain_one + shift_one).astype(jnp.bfloat16)
    projected = (product(first_norm, qkv_mat) + qkv_bias).astype(jnp.bfloat16)
    context, stats = attend(projected, segment)
    residual = inputs + (product(context, dense_mat) + dense_bias)
    unit_two, scale_two = norm_parts(residual)
    second_norm = (unit_two * gain_two + shift_two).astype(jnp.bfloat16)
    expanded = product(second_norm, expand_mat) + expand_bias
    activated_wide, bend = gelu_both(expanded)
    activated = activated_wide.astype(jnp.bfloat16)
    grad_contract = scatter(outer_sum(activated, grad_low))
    result = residual + (product(activated, contract_mat) + contract_bias)

    grad_expanded = (times_transposed(grad_low, contract_mat) * bend).astype(jnp.bfloat16)
    grad_expand = scatter(outer_sum(second_norm, grad_expanded))
    grad_second = times_transposed(grad_expanded, expand_mat)
    grad_mixed = grad_out + norm_back(unit_two, scale_two, gain_two, grad_second)
    grad_attn = grad_mixed.astype(jnp.bfloat16)
    grad_dense = scatter(outer_sum(context, grad_attn))
    grad_context = times_transposed(grad_attn, dense_mat).astype(jnp.bfloat16)
    grad_parts = attend_back(projected, grad_context, stats, segment)
    grad_projected = jnp.concatenate(grad_parts, axis=1)
    grad_joined = scatter(outer_sum(first_norm, grad_projected))
    grad_first = times_transposed(grad_projected, qkv_mat)
    input_grad = grad_mixed + norm_back(unit_one, scale_one, gain_one, grad_first)
    grad_vector = jnp.concatenate(
        [
            jnp.sum(grad_first * unit_one, axis=0),
            jnp.sum(grad_first, axis=0),
            jnp.sum(grad_projected.astype(jnp.float32), axis=0),
            jnp.sum(grad_mixed, axis=0),
            jnp.sum(grad_second * unit_two, axis=0),
            jnp.sum(grad_second, axis=0),
            jnp.sum(grad_expanded.astype(jnp.float32), axis=0),
            jnp.sum(grad_out, axis=0),
        ]
    )
    vector_grad = lax.psum(
        lax.psum_scatter(grad_vector, "fsdp", scatter_dimension=0, tiled=True), "dp"
    )

    qkv_new, qkv_first_new, qkv_second_new = adam_update(
        qkv_weight, qkv_first, qkv_second, grad_joined, matrix_rate, decay_rate
    )
    dense_new, dense_first_new, dense_second_new = adam_update(
        dense_weight, dense_first, dense_second, grad_dense, matrix_rate, decay_rate
    )
    expand_new, expand_first_new, expand_second_new = adam_update(
        expand_weight, expand_first, expand_second, grad_expand, matrix_rate, decay_rate
    )
    contract_new, contract_first_new, contract_second_new = adam_update(
        contract_weight, contract_first, contract_second, grad_contract, matrix_rate, decay_rate
    )
    vectors_new, vector_first_new, vector_second_new = adam_update(
        vectors, vector_first, vector_second, vector_grad, vector_rate, 0.0
    )
    return (
        result.astype(jnp.bfloat16).reshape(tokens.shape),
        input_grad.reshape(tokens.shape),
        qkv_new,
        dense_new,
        expand_new,
        contract_new,
        vectors_new,
        qkv_first_new,
        dense_first_new,
        expand_first_new,
        contract_first_new,
        vector_first_new,
        qkv_second_new,
        dense_second_new,
        expand_second_new,
        contract_second_new,
        vector_second_new,
    )


def solution(mesh):
    return jax.shard_map(
        local,
        mesh=mesh,
        in_specs=(
            P(None, ("fsdp", "dp"), None),
            P(None, ("fsdp", "dp"), None),
            P(None, ("fsdp", "dp")),
            P("fsdp", None),
            P("fsdp", None),
            P("fsdp", None),
            P("fsdp", None),
            P("fsdp"),
            P("fsdp", None),
            P("fsdp", None),
            P("fsdp", None),
            P("fsdp", None),
            P("fsdp"),
            P("fsdp", None),
            P("fsdp", None),
            P("fsdp", None),
            P("fsdp", None),
            P("fsdp"),
        ),
        out_specs=(
            P(None, ("fsdp", "dp"), None),
            P(None, ("fsdp", "dp"), None),
            P("fsdp", None),
            P("fsdp", None),
            P("fsdp", None),
            P("fsdp", None),
            P("fsdp"),
            P("fsdp", None),
            P("fsdp", None),
            P("fsdp", None),
            P("fsdp", None),
            P("fsdp"),
            P("fsdp", None),
            P("fsdp", None),
            P("fsdp", None),
            P("fsdp", None),
            P("fsdp"),
        ),
        check_vma=False,
    )
```

```python
import functools

import jax
import jax.numpy as jnp
from jax import lax
from jax.experimental import pallas as pl
from jax.experimental.pallas import tpu as pltpu
from jax.sharding import PartitionSpec as P

HEADS = 16
HEAD_DIM = 64
D = 1024
FF = 4096
STEP = 10
VEC = 13312

norm_eps = 1e-05
beta_first = 0.9
beta_second = 0.95
adam_eps = 1e-08
matrix_rate = 0.05
vector_rate = 0.5
decay_rate = 0.1
excluded = 1e33
TILE = 256
PAIR = 2


def pieces(vector):
    return (
        vector[0:D],
        vector[D : 2 * D],
        vector[2 * D : 5 * D],
        vector[5 * D : 6 * D],
        vector[6 * D : 7 * D],
        vector[7 * D : 8 * D],
        vector[8 * D : 8 * D + FF],
        vector[8 * D + FF : 9 * D + FF],
    )


def product(left_side, right_side):
    return jnp.dot(left_side, right_side, preferred_element_type=jnp.float32)


def outer_sum(left_side, right_side):
    return lax.dot_general(
        left_side, right_side, (((0,), (0,)), ((), ())), preferred_element_type=jnp.float32
    )


def times_transposed(left_side, right_side):
    return lax.dot_general(
        left_side, right_side, (((1,), (1,)), ((), ())), preferred_element_type=jnp.float32
    )


def norm_parts(inputs):
    average = jnp.mean(inputs, axis=-1, keepdims=True)
    centered = inputs - average
    spread = jnp.mean(centered * centered, axis=-1, keepdims=True)
    scale = lax.rsqrt(spread + norm_eps)
    return centered * scale, scale


def norm_back(unit, scale, gain, upstream):
    by_gain = upstream * gain
    mean_one = jnp.mean(by_gain, axis=-1, keepdims=True)
    mean_two = jnp.mean(by_gain * unit, axis=-1, keepdims=True)
    return scale * (by_gain - mean_one - unit * mean_two)


def gelu_both(values):
    root = 0.7978845608028654
    square = values * values
    bent = jnp.tanh(root * values * (1.0 + 0.044715 * square))
    half = 0.5 * (1.0 + bent)
    slope = half + 0.5 * values * (1.0 - bent * bent) * root * (1.0 + 3 * 0.044715 * square)
    return values * half, slope


def slope_of(head):
    return jnp.exp2(-8.0 * (head.astype(jnp.float32) + 1.0) / HEADS)


def fill_distance(seg_col, seg_row, distance_ref):
    rows = distance_ref.shape[0]
    key_rows = lax.broadcasted_iota(jnp.int32, (rows, rows), 0)
    query_rows = lax.broadcasted_iota(jnp.int32, (rows, rows), 1)
    allowed = (seg_col == seg_row) & (key_rows <= query_rows)
    distance_ref[...] = jnp.where(allowed, (query_rows - key_rows).astype(jnp.float32), excluded)


def attend_kernel(seg_col, seg_row, q_ref, k_ref, v_ref, out_ref, stat_ref, distance_ref):
    step = pl.program_id(1)

    @pl.when(step == 0)
    def _():
        fill_distance(seg_col[0], seg_row[0], distance_ref)

    rows = q_ref.shape[0]
    queries = q_ref[...] * jnp.bfloat16(HEAD_DIM**-0.5)
    values_turned = v_ref[...].T
    for local_head in range(PAIR):
        slope = slope_of(step * PAIR + local_head)
        lanes = slice(local_head * HEAD_DIM, (local_head + 1) * HEAD_DIM)
        for tile in range(rows // TILE):
            high = (tile + 1) * TILE
            span = slice(tile * TILE, high)
            scores = times_transposed(k_ref[:high, lanes], queries[span, lanes])
            scores = scores - slope * distance_ref[:high, span]
            top = jnp.max(scores, axis=0, keepdims=True)
            exponent = jnp.exp(scores - top)
            total = jnp.sum(exponent, axis=0, keepdims=True)
            probability = (exponent * (1.0 / total)).astype(jnp.bfloat16)
            turned = product(values_turned[lanes, :high], probability)
            out_ref[span, lanes] = turned.T.astype(jnp.bfloat16)
            stat_ref[0, local_head : local_head + 1, span] = top + jnp.log(total)


def attend_back_kernel(
    seg_col, seg_row, q_ref, k_ref, v_ref, up_ref, stat_ref, dq_ref, dk_ref, dv_ref,
    distance_ref, sum_k, sum_v,
):
    step = pl.program_id(1)

    @pl.when(step == 0)
    def _():
        fill_distance(seg_col[0], seg_row[0], distance_ref)

    rows = q_ref.shape[0]
    queries = q_ref[...] * jnp.bfloat16(HEAD_DIM**-0.5)
    upstream = up_ref[...]
    keys_turned = k_ref[...].T
    for local_head in range(PAIR):
        slope = slope_of(step * PAIR + local_head)
        lanes = slice(local_head * HEAD_DIM, (local_head + 1) * HEAD_DIM)
        for tile in range(rows // TILE):
            high = (tile + 1) * TILE
            span = slice(tile * TILE, high)
            scores = times_transposed(k_ref[:high, lanes], queries[span, lanes])
            scores = scores - slope * distance_ref[:high, span]
            probability = jnp.exp(scores - stat_ref[0, local_head : local_head + 1, span])
            grad_probs = times_transposed(v_ref[:high, lanes], upstream[span, lanes])
            weighted = probability * grad_probs
            correction = jnp.sum(weighted, axis=0, keepdims=True)
            grad_scores = (weighted - probability * correction).astype(jnp.bfloat16)
            grad_query = product(keys_turned[lanes, :high], grad_scores)
            dq_ref[span, lanes] = (grad_query.T * HEAD_DIM**-0.5).astype(jnp.bfloat16)
            part_k = product(grad_scores, queries[span, lanes])
            part_v = product(probability.astype(jnp.bfloat16), upstream[span, lanes])
            if tile == 0:
                sum_k[:high, lanes] = part_k
                sum_v[:high, lanes] = part_v
            else:
                low = tile * TILE
                sum_k[:low, lanes] += part_k[:low]
                sum_v[:low, lanes] += part_v[:low]
                sum_k[low:high, lanes] = part_k[low:]
                sum_v[low:high, lanes] = part_v[low:]
    dk_ref[...] = sum_k[...].astype(jnp.bfloat16)
    dv_ref[...] = sum_v[...].astype(jnp.bfloat16)


def attention_specs(rows, blocks):
    steps = HEADS // PAIR
    width = PAIR * HEAD_DIM
    seg_specs = [
        pl.BlockSpec((1, rows, 1), lambda b, s: (b, 0, 0)),
        pl.BlockSpec((1, 1, rows), lambda b, s: (b, 0, 0)),
    ]

    part = pl.BlockSpec((rows, width), lambda b, s: (b, s))
    stat = pl.BlockSpec((1, PAIR, rows), lambda b, s: (b * steps + s, 0, 0))
    return steps, seg_specs, part, stat


def attend(projected, segment):
    blocks, rows = segment.shape
    steps, seg_specs, part, stat = attention_specs(rows, blocks)
    return pl.pallas_call(
        attend_kernel,
        grid=(blocks, steps),
        in_specs=seg_specs + [part, part, part],
        out_specs=[part, stat],
        out_shape=[
            jax.ShapeDtypeStruct((blocks * rows, D), jnp.bfloat16),
            jax.ShapeDtypeStruct((blocks * steps, PAIR, rows), jnp.float32),
        ],
        scratch_shapes=[pltpu.VMEM((rows, rows), jnp.float32)],
        compiler_params=pltpu.CompilerParams(vmem_limit_bytes=32 * 2**20),
        cost_estimate=pl.CostEstimate(
            flops=blocks * HEADS * rows * rows * HEAD_DIM * 8,
            bytes_accessed=blocks * rows * D * 8,
            transcendentals=blocks * HEADS * rows * rows,
        ),
        name="attend",
    )(segment[:, :, None], segment[:, None, :], *projected)


def attend_back(projected, upstream, stats, segment):
    blocks, rows = segment.shape
    steps, seg_specs, part, stat = attention_specs(rows, blocks)
    width = PAIR * HEAD_DIM
    return pl.pallas_call(
        attend_back_kernel,
        grid=(blocks, steps),
        in_specs=seg_specs + [part, part, part, part, stat],
        out_specs=[part, part, part],
        out_shape=[jax.ShapeDtypeStruct((blocks * rows, D), jnp.bfloat16)] * 3,
        scratch_shapes=[
            pltpu.VMEM((rows, rows), jnp.float32),
            pltpu.VMEM((rows, width), jnp.float32),
            pltpu.VMEM((rows, width), jnp.float32),
        ],
        compiler_params=pltpu.CompilerParams(vmem_limit_bytes=32 * 2**20),
        cost_estimate=pl.CostEstimate(
            flops=blocks * HEADS * rows * rows * HEAD_DIM * 20,
            bytes_accessed=blocks * rows * D * 14,
            transcendentals=blocks * HEADS * rows * rows,
        ),
        name="attend_back",
    )(segment[:, :, None], segment[:, None, :], *projected, upstream, stats)


def adam_update(weight, first, second, grad, rate, decay):
    new_first = beta_first * first + (1.0 - beta_first) * grad
    new_second = beta_second * second + (1.0 - beta_second) * grad * grad
    corrected_first = new_first / (1.0 - beta_first**STEP)
    corrected_second = new_second / (1.0 - beta_second**STEP)
    new_weight = weight - rate * (
        corrected_first / (jnp.sqrt(corrected_second) + adam_eps) + decay * weight
    )
    return (new_weight, new_first, new_second)


def links(turn):
    count = lax.axis_size("fsdp").bit_length() - 1
    near = min(3, count)
    bits = [(turn + at) % near for at in range(near)] + list(range(near, count))
    return bits, list(range(count))


def exchange(values, axis, bit):
    size = lax.axis_size(axis)
    return lax.ppermute(values, axis, [(at, at ^ (1 << bit)) for at in range(size)])


def joined(mine, theirs, place, axis):
    first = jnp.where(place == 0, mine, theirs)
    second = jnp.where(place == 0, theirs, mine)
    return jnp.stack((first, second), axis=axis)


class Gather:
    def __init__(self, own, turn):
        self.copy = lax.axis_index("dp")
        self.bits = list(reversed(links(turn)[0]))
        self.have = []
        self.rest = own.shape[1:]
        share = own.shape[0] // 2
        self.held = lax.dynamic_slice_in_dim(own, self.copy * share, share, 0).astype(jnp.bfloat16)

    def step(self):
        bit = self.bits.pop(0)
        place = (lax.axis_index("fsdp") >> bit) & 1
        axis = sum(1 for other in self.have if other > bit)
        self.held = joined(self.held, exchange(self.held, "fsdp", bit), place, axis)
        self.have.append(bit)

    def finish(self):
        while self.bits:
            self.step()
        held = joined(self.held, exchange(self.held, "dp", 0), self.copy, len(self.have))
        return held.reshape((-1,) + self.rest)


class Scatter:
    def __init__(self, total, turn):
        self.bits, self.left = links(turn)
        self.rest = total.shape[1:]
        self.wide = total.dtype
        count = len(self.left)
        share = total.shape[0] // 2 ** (count + 1)
        self.held = total.reshape((2,) * (count + 1) + (share,) + self.rest)
        self.halve(lax.axis_index("dp"), count, "dp", 0)

    def halve(self, place, axis, name, bit):
        keep = lax.dynamic_index_in_dim(self.held, place, axis, keepdims=False)
        give = lax.dynamic_index_in_dim(self.held, 1 - place, axis, keepdims=False)
        taken = exchange(give, name, bit)
        self.held = (keep.astype(jnp.float32) + taken.astype(jnp.float32)).astype(self.wide)

    def step(self):
        if self.bits:
            bit = self.bits.pop(0)
            axis = sum(1 for other in self.left if other > bit)
            self.halve((lax.axis_index("fsdp") >> bit) & 1, axis, "fsdp", bit)
            self.left.remove(bit)

    def finish(self):
        while self.bits:
            self.step()
        held = joined(self.held, exchange(self.held, "dp", 0), lax.axis_index("dp"), 0)
        return held.reshape((-1,) + self.rest).astype(jnp.float32)


def tie(values, chains):
    tied, helds = lax.optimization_barrier((values, tuple(chain.held for chain in chains)))
    for chain, held in zip(chains, helds):
        chain.held = held
    return tied


def scatter_parts(left_side, right_side, turns):
    width = right_side.shape[1] // len(turns)
    return [
        Scatter(
            outer_sum(left_side, right_side[:, at * width : (at + 1) * width]).astype(jnp.bfloat16),
            turn,
        )
        for at, turn in enumerate(turns)
    ]


def finish_all(chains):
    return jnp.concatenate([chain.finish() for chain in chains], axis=1)


def local(
    tokens,
    cotangent,
    lengths,
    qkv_weight,
    dense_weight,
    expand_weight,
    contract_weight,
    vectors,
    qkv_first,
    dense_first,
    expand_first,
    contract_first,
    vector_first,
    qkv_second,
    dense_second,
    expand_second,
    contract_second,
    vector_second,
):
    batches, row_count, _ = tokens.shape
    rows = batches * row_count
    bounds = jnp.cumsum(lengths, axis=1)
    row_ids = jnp.arange(row_count, dtype=jnp.int32)
    segment = jnp.sum((row_ids[None, :, None] >= bounds[:, None, :]).astype(jnp.int32), axis=2)
    inside = (row_ids[None, :] < bounds[:, -1:]).reshape(rows, 1)

    vector_chain = Gather(vectors, 0)
    qkv_chains = [Gather(qkv_weight[:, at * D : (at + 1) * D], at) for at in range(3)]
    dense_chain = Gather(dense_weight, 0)
    expand_chain = Gather(expand_weight, 1)
    contract_chain = Gather(contract_weight, 2)
    vector_all = vector_chain.finish()
    qkv_mats = tuple(chain.finish() for chain in qkv_chains)
    wide_chains = [dense_chain, expand_chain, contract_chain]
    for chain in wide_chains:
        while len(chain.bits) > 1:
            chain.step()
    qkv_mats = tie(qkv_mats, wide_chains)
    (
        gain_one, shift_one, qkv_bias, dense_bias, gain_two, shift_two, expand_bias, contract_bias,
    ) = pieces(vector_all.astype(jnp.float32))

    inputs = tokens.reshape(rows, D).astype(jnp.float32)
    grad_low = jnp.where(inside, cotangent.reshape(rows, D), jnp.bfloat16(0))
    grad_out = grad_low.astype(jnp.float32)

    unit_one, scale_one = norm_parts(inputs)
    first_norm = (unit_one * gain_one + shift_one).astype(jnp.bfloat16)
    projected = tuple(
        (product(first_norm, mat) + qkv_bias[at * D : (at + 1) * D]).astype(jnp.bfloat16)
        for at, mat in enumerate(qkv_mats)
    )
    context, stats = attend(projected, segment)
    for chain in wide_chains:
        chain.step()
    context = tie(context, wide_chains)
    dense_mat = dense_chain.finish()
    expand_mat = expand_chain.finish()
    contract_mat = contract_chain.finish()
    residual = inputs + (product(context, dense_mat) + dense_bias)
    unit_two, scale_two = norm_parts(residual)
    second_norm = (unit_two * gain_two + shift_two).astype(jnp.bfloat16)
    expanded = product(second_norm, expand_mat) + expand_bias
    activated_wide, bend = gelu_both(expanded)
    activated = activated_wide.astype(jnp.bfloat16)
    contract_grads = scatter_parts(activated, grad_low, (0, 1))
    activated, grad_held = tie((activated, grad_low), contract_grads)
    result = residual + (product(activated, contract_mat) + contract_bias)

    grad_expanded = (times_transposed(grad_held, contract_mat) * bend).astype(jnp.bfloat16)
    for chain in contract_grads:
        chain.step()
    grad_expanded = tie(grad_expanded, contract_grads)
    expand_grads = scatter_parts(second_norm, grad_expanded, (2, 0))
    for chain in contract_grads:
        chain.step()
    grad_expanded = tie(grad_expanded, contract_grads + expand_grads)
    grad_second = times_transposed(grad_expanded, expand_mat)
    grad_mixed = grad_out + norm_back(unit_two, scale_two, gain_two, grad_second)
    grad_attn = grad_mixed.astype(jnp.bfloat16)
    dense_grads = scatter_parts(context, grad_attn, (1,))
    grad_context = times_transposed(grad_attn, dense_mat).astype(jnp.bfloat16)
    for chain in contract_grads:
        chain.step()
    grad_context = tie(grad_context, contract_grads + expand_grads + dense_grads)
    grad_parts = attend_back(projected, grad_context, stats, segment)
    for chain in contract_grads + expand_grads + dense_grads:
        chain.step()
    for chain in expand_grads + dense_grads:
        chain.step()
    grad_parts = tie(tuple(grad_parts), contract_grads + expand_grads + dense_grads)
    qkv_grads = [
        scatter_parts(first_norm, part, (turn,))[0] for turn, part in enumerate(grad_parts)
    ]
    grad_parts = tie(grad_parts, qkv_grads)
    grad_first = sum(times_transposed(part, mat) for part, mat in zip(grad_parts, qkv_mats))
    input_grad = grad_mixed + norm_back(unit_one, scale_one, gain_one, grad_first)
    grad_vector = jnp.concatenate(
        [
            jnp.sum(grad_first * unit_one, axis=0),
            jnp.sum(grad_first, axis=0),
            *[jnp.sum(part.astype(jnp.float32), axis=0) for part in grad_parts],
            jnp.sum(grad_mixed, axis=0),
            jnp.sum(grad_second * unit_two, axis=0),
            jnp.sum(grad_second, axis=0),
            jnp.sum(grad_expanded.astype(jnp.float32), axis=0),
            jnp.sum(grad_out, axis=0),
        ]
    )
    vector_grad = Scatter(grad_vector, 0).finish()
    grad_contract = finish_all(contract_grads)
    grad_expand = finish_all(expand_grads)
    grad_dense = finish_all(dense_grads)
    grad_joined = finish_all(qkv_grads)

    qkv_new, qkv_first_new, qkv_second_new = adam_update(
        qkv_weight, qkv_first, qkv_second, grad_joined, matrix_rate, decay_rate
    )
    dense_new, dense_first_new, dense_second_new = adam_update(
        dense_weight, dense_first, dense_second, grad_dense, matrix_rate, decay_rate
    )
    expand_new, expand_first_new, expand_second_new = adam_update(
        expand_weight, expand_first, expand_second, grad_expand, matrix_rate, decay_rate
    )
    contract_new, contract_first_new, contract_second_new = adam_update(
        contract_weight, contract_first, contract_second, grad_contract, matrix_rate, decay_rate
    )
    vectors_new, vector_first_new, vector_second_new = adam_update(
        vectors, vector_first, vector_second, vector_grad, vector_rate, 0.0
    )
    return (
        result.astype(jnp.bfloat16).reshape(tokens.shape),
        input_grad.reshape(tokens.shape),
        qkv_new,
        dense_new,
        expand_new,
        contract_new,
        vectors_new,
        qkv_first_new,
        dense_first_new,
        expand_first_new,
        contract_first_new,
        vector_first_new,
        qkv_second_new,
        dense_second_new,
        expand_second_new,
        contract_second_new,
        vector_second_new,
    )


def solution(mesh):
    return jax.shard_map(
        local,
        mesh=mesh,
        in_specs=(
            P(None, ("fsdp", "dp"), None),
            P(None, ("fsdp", "dp"), None),
            P(None, ("fsdp", "dp")),
            P("fsdp", None),
            P("fsdp", None),
            P("fsdp", None),
            P("fsdp", None),
            P("fsdp"),
            P("fsdp", None),
            P("fsdp", None),
            P("fsdp", None),
            P("fsdp", None),
            P("fsdp"),
            P("fsdp", None),
            P("fsdp", None),
            P("fsdp", None),
            P("fsdp", None),
            P("fsdp"),
        ),
        out_specs=(
            P(None, ("fsdp", "dp"), None),
            P(None, ("fsdp", "dp"), None),
            P("fsdp", None),
            P("fsdp", None),
            P("fsdp", None),
            P("fsdp", None),
            P("fsdp"),
            P("fsdp", None),
            P("fsdp", None),
            P("fsdp", None),
            P("fsdp", None),
            P("fsdp"),
            P("fsdp", None),
            P("fsdp", None),
            P("fsdp", None),
            P("fsdp", None),
            P("fsdp"),
        ),
        check_vma=False,
    )
```
